768 devices in a mesh: blk: 32 (over y, z_hi, core), rep: 24 (over z_lo, x).
Axes of the slice: x: 4, y: 8, z: 12 (z_hi: 2, z_lo: 6; z = z_hi * 6 + z_lo), core: 2. Of those that a mesh axis runs over, the one named last changes fastest.
Arguments:
- features: bfloat16 [98304, 256], P('blk'), may hold values from -6 to 6
- tiles: bfloat16 [32, 32, 24, 4, 128, 128], P('blk', None, 'rep'), may hold values from -0.06591797 to 0.06591797
- tile_rows: int32 [32, 32, 24, 4], P('blk', None, 'rep'), may hold values from 0 to 23
- tile_count: int32 [32, 32, 24], P('blk', None, 'rep'), may hold values from 1 to 4, as said below
- weight: bfloat16 [256, 256], replicated, may hold values from -0.375 to 0.375
- cotangent: bfloat16 [98304, 256], P('blk'), may hold values from -6 to 6
Outputs:
- activation: bfloat16 [98304, 256], P(('blk', 'rep'))
- grad_features: bfloat16 [98304, 256], P(('blk', 'rep'))
- grad_weight: float32 [256, 256], replicated
The draws below stay inside these ranges and needn't reach their ends.
Inputs may be any that keep to these rules, and one draw needn't show every extreme that they name: `tile_count`: each live count is 1 to 4; the pair of a row block with itself has 4 in every column part.
All inputs are finite; a program needn't handle non-finite values.
Results may differ from the reference program's by a relative error of at most 0.035.
Values may be sent and summed in bfloat16 or wider, within the bound.
A program may use at most 64 MiB of HBM per device.

```python
import jax
import jax.numpy as jnp
from jax import lax

F = 256
TILE = 128
K = 4
NODES = 98304
N_BLK = 32
N_REP = 24


def draw_tile_count(key, part):
    key = jax.random.fold_in(key, 7)
    key_heavy, key_light, key_full = jax.random.split(key, 3)
    shape = (N_BLK, N_BLK, N_REP)
    heavy = jax.random.randint(key_heavy, (N_BLK, 1, 1), 0, 4) == 0
    light_count = jax.random.randint(key_light, shape, 1, K // 2 + 1)
    full_count = jax.random.randint(key_full, shape, 1, K + 1)
    counts = jnp.where(heavy, full_count, light_count)
    same = jnp.arange(N_BLK)[:, None, None] == jnp.arange(N_BLK)[None, :, None]
    return jnp.where(same, K, counts).astype(jnp.int32)


def plant(result, key, low, top_value):
    index_at = [jax.random.randint(jax.random.fold_in(key, axis), (), 0, length) for axis, length in enumerate(result.shape)]
    main_axis = result.shape.index(max(result.shape))
    beside = index_at[:main_axis] + [(index_at[main_axis] + 1) % result.shape[main_axis]] + index_at[main_axis + 1:]
    return result.at[tuple(index_at)].set(low).at[tuple(beside)].set(top_value)


def block_levels(rng, extent, pieces, low, top_value):
    level, own = 1.0, jax.random.fold_in(rng, 6)
    for axis_at, blocks in pieces:
        draws = jnp.exp(jax.random.uniform(jax.random.fold_in(own, axis_at), (blocks,), jnp.float32, low / len(pieces), top_value / len(pieces)))
        level = level * jnp.repeat(draws, extent[axis_at] // blocks).reshape([-1 if axis == axis_at else 1 for axis in range(len(extent))])
    return level


def noise(key, dims, deviation, most, cuts=(), held_as=jnp.bfloat16):
    level = block_levels(key, dims, cuts, -0.22, 0.18) if cuts else 1.0
    entries = jax.random.normal(key, dims, jnp.float32) * deviation * level
    return jnp.minimum(jnp.maximum(entries, -most), most).astype(held_as)


def setup_inputs(seed: int = 0) -> dict:
    key_of = jax.random.split(jax.random.key(seed), 7)
    features = noise(key_of[0], (NODES, F), 1.0, 6.0, ((0, 32),))
    tiles = noise(key_of[1], (N_BLK, N_BLK, N_REP, K, TILE, TILE), ((2.0 / (N_BLK * K * TILE)) ** 0.5), 0.06591797, ((0, 32), (2, 24)))
    tile_rows = plant(jax.random.randint(key_of[2], (N_BLK, N_BLK, N_REP, K), 0, N_REP), jax.random.fold_in(key_of[2], 1), 0, N_REP - 1).astype(jnp.int32)
    tile_count = draw_tile_count(jax.random.fold_in(key_of[6], 71), 0)
    weight = noise(key_of[4], (F, F), F ** -0.5, 0.375)
    cotangent = noise(key_of[5], (NODES, F), 1.0, 6.0, ((0, 32),))
    return dict(features=features, tiles=tiles, tile_rows=tile_rows, tile_count=tile_count, weight=weight, cotangent=cotangent)


def masks(tile_rows, tile_count, b, r):
    slots = jnp.arange(K, dtype=jnp.int32)
    live = slots[None, :] < tile_count[b, :, r][:, None]
    hits = tile_rows[b, :, r][:, :, None] == jnp.arange(N_REP, dtype=jnp.int32)[None, None, :]
    return (hits & live[:, :, None]).astype(jnp.float32)


def to_bf16_back(value):
    return lax.optimization_barrier(value.astype(jnp.bfloat16)).astype(jnp.float32)


def reference(features, tiles, tile_rows, tile_count, weight, cotangent):
    xs = features.reshape(N_BLK, N_REP, TILE, F).astype(jnp.float32)

    def fwd_block(b):
        def fwd_part(r):
            local = tiles[b, :, r].astype(jnp.float32)
            place = masks(tile_rows, tile_count, b, r)
            prod = jnp.einsum("ckij,cjf->ckif", local, xs[:, r])
            return to_bf16_back(jnp.einsum("ckt,ckif->tif", place, prod))
        return jnp.sum(lax.map(fwd_part, jnp.arange(N_REP)), axis=0)

    summed = lax.map(fwd_block, jnp.arange(N_BLK)).reshape(NODES, F)
    aggregate = summed.astype(jnp.bfloat16)
    pre = jnp.dot(aggregate, weight, preferred_element_type=jnp.float32)
    sig = jax.nn.sigmoid(pre)
    activation = (pre * sig).astype(jnp.bfloat16)
    dpre = (cotangent.astype(jnp.float32) * sig * (1.0 + pre * (1.0 - sig))).astype(jnp.bfloat16)
    grad_weight = jnp.dot(aggregate.T, dpre, preferred_element_type=jnp.float32)
    back = jnp.dot(dpre, weight.T, preferred_element_type=jnp.float32).astype(jnp.bfloat16)
    ys = back.reshape(N_BLK, N_REP, TILE, F)

    def bwd_block(total, b):
        rows_here = ys[b].astype(jnp.float32)

        def bwd_part(r):
            local = tiles[b, :, r].astype(jnp.float32)
            place = masks(tile_rows, tile_count, b, r)
            picked = jnp.einsum("ckt,tif->ckif", place, rows_here)
            return to_bf16_back(jnp.einsum("ckij,ckif->cjf", local, picked))
        terms = lax.map(bwd_part, jnp.arange(N_REP))
        return total + jnp.swapaxes(terms, 0, 1), None

    start_total = jnp.zeros((N_BLK, N_REP, TILE, F), jnp.float32)
    total = lax.scan(bwd_block, start_total, jnp.arange(N_BLK))[0]
    grad_features = total.reshape(NODES, F).astype(jnp.bfloat16)
    return activation, grad_features, grad_weight
```

```python
import functools

import jax
import jax.numpy as jnp
from jax import lax
from jax.experimental import pallas as pl
from jax.experimental.pallas import tpu as pltpu
from jax.sharding import PartitionSpec as P

NX, NY, NZ = 4, 8, 6
SIDE, WIDTH, PARTS, BLOCKS, SLOTS = 128, 256, 24, 32, 4
MESH = pl.DeviceIdType.MESH
BF, F32 = jnp.bfloat16, jnp.float32
VMEM = pl.BlockSpec(memory_space=pltpu.VMEM)
SMEM = pl.BlockSpec(memory_space=pltpu.SMEM)
ANY = pl.BlockSpec(memory_space=pl.ANY)


class Place:
    def __init__(self):
        self.b = lax.axis_index("blk")
        self.r = lax.axis_index("rep")
        self.y = lax.div(self.b, 4)
        self.h = lax.rem(lax.div(self.b, 2), 2)
        self.c = lax.rem(self.b, 2)
        self.z = lax.div(self.r, NX)
        self.x = lax.rem(self.r, NX)

    def blk(self, dy=0, e=0, flip=0):
        y = lax.rem(self.y + dy + NY, NY)
        h = 1 - self.h if e else self.h
        c = 1 - self.c if flip else self.c
        return (y * 2 + h) * 2 + c

    def rep(self, dz=0, dx=0):
        return lax.rem(self.z + dz + NZ, NZ) * NX + lax.rem(self.x + dx + NX, NX)


def greet(peers):
    barrier = pltpu.get_barrier_semaphore()
    for peer in peers:
        pl.semaphore_signal(barrier, inc=1, device_id=peer, device_id_type=MESH)
    pl.semaphore_wait(barrier, len(peers))


def remote(src, dst, send_sem, recv_sem, device):
    return pltpu.make_async_remote_copy(
        src_ref=src, dst_ref=dst, send_sem=send_sem, recv_sem=recv_sem,
        device_id=device, device_id_type=MESH,
    )


def gather_kernel(feat, out, send_sem, recv_sem, own_sem):
    me = Place()
    sibling = (me.blk(flip=1), me.r)
    up, down = (me.blk(dy=1), me.r), (me.blk(dy=-1), me.r)
    far = me.rep(dz=3)
    partner = (me.blk(e=1), far)
    greet([sibling, up, down, partner])
    sends = []

    def start(src, slot, lane, device):
        copy = remote(src, out.at[slot], send_sem.at[len(sends)], recv_sem.at[slot], device)
        copy.start()
        sends.append(copy)

    def arrive(slot):
        remote(out.at[slot], out.at[slot], send_sem.at[0], recv_sem.at[slot], sibling).wait_recv()

    own = feat.at[pl.ds(me.r * SIDE, SIDE), :]
    start(feat.at[pl.ds(far * SIDE, SIDE), :], me.b, 0, partner)
    start(own, me.b, 1, up)
    start(own, me.b, 2, down)
    start(own, me.b, 3, sibling)
    local = pltpu.make_async_copy(own, out.at[me.b], own_sem)
    local.start()
    crossed = me.blk(e=1)
    arrive(crossed)
    start(out.at[crossed], crossed, 0, up)
    start(out.at[crossed], crossed, 1, down)
    start(out.at[crossed], crossed, 2, sibling)
    for far_y in (1, 2, 3, 4):
        for e in (0, 1):
            for sign, onward, reach in ((-1, up, 3 + e), (1, down, 4 - e)):
                if far_y > reach:
                    continue
                slot = me.blk(dy=sign * far_y, e=e)
                arrive(slot)
                if far_y < reach:
                    start(out.at[slot], slot, 0, onward)
                start(out.at[slot], slot, 1, sibling)
    local.wait()
    for dy in range(NY):
        for e in (0, 1):
            arrive(me.blk(dy=dy, e=e, flip=1))
    for copy in sends:
        copy.wait_send()


GATHER_SENDS = 4 + 3 + 14 + 12


def forward_kernel(index, tiles, feats, out, total):
    total[...] = jnp.zeros_like(total)

    def column(c, carry):
        x = feats[c]
        for k in range(SLOTS):
            t = index[c * SLOTS + k]

            @pl.when(t < PARTS)
            def _():
                total[t] += jnp.dot(tiles[c, k], x, preferred_element_type=F32)

        return carry

    lax.fori_loop(0, BLOCKS, column, 0)
    out[...] = total[...].astype(BF)


Z_ORDER = (3, 2, 4, 1, 5, 0)


def group_of(p):
    m, e = 4 - lax.div(p, 4), 1 - lax.rem(p, 2)
    dy = jnp.where(lax.rem(p, 4) < 2, m, -m)
    return dy, e


GROUPS = [(m if p % 4 < 2 else -m, 1 - p % 2) for p in range(2, 18) for m in [4 - p // 4]]
HOPS = [(sign, e, m) for m in (4, 3, 2, 1) for e in (1, 0) for sign in (1, -1)
        if m <= (3 + e if sign > 0 else 4 - e)]


def back_kernel(
    index, part, tiles_hbm, weight, cot_hbm,
    act_out, grad_out, weight_out,
    tiles, cot, got_x, sum_z, got_z, back, to_core, from_core, mine, ring_out, ring_in,
    cross_out, cross_in, wsum, w1_out, w1_in, w2_out, w2_in, w3_out, w3_in, w4_out, w4_in, w5_in, w6_in,
    local_sem, rx_s, rx_r, rz_s, rz_r, gz_s, gz_r, gx_s, gx_r, core_s, core_r, ring_s, ring_r,
    cross_s, cross_r, wa_s, wa_r, wy_s, wy_r, wx_s, wx_r, wz_s, wz_r, wo_s, wo_r,
):
    me = Place()
    sibling = (me.blk(flip=1), me.r)
    up, down = (me.blk(dy=1), me.r), (me.blk(dy=-1), me.r)
    other = (me.blk(e=1), me.r)
    peers = [sibling]
    peers += [(me.blk(dy=dy), me.r) for dy in range(1, NY)]
    peers += [(me.b, me.rep(dx=dx)) for dx in range(1, NX)]
    peers += [(me.blk(e=e), me.rep(dz=dz)) for e in (0, 1) for dz in range(NZ) if e or dz]

    load_tiles = pltpu.make_async_copy(tiles_hbm.at[0, :, 0], tiles, local_sem.at[0])
    load_tiles.start()
    load_cot = pltpu.make_async_copy(cot_hbm.at[pl.ds(me.r * SIDE, SIDE), :], cot, local_sem.at[1])
    load_cot.start()
    greet(peers)
    sends = []

    def start(*args):
        copy = remote(*args)
        copy.start()
        sends.append(copy)

    def arrive(dst, sem):
        remote(dst, dst, local_sem.at[2], sem, sibling).wait_recv()

    for o in Z_ORDER:
        for dx in (1, 3, 2):
            start(part.at[me.rep(dz=o, dx=dx)], got_x.at[o, dx], rx_s.at[o, dx], rx_r.at[o, dx],
                  (me.b, me.rep(dx=dx)))
    for o in Z_ORDER:
        value = part[me.rep(dz=o)].astype(F32)
        for dx in (1, 3, 2):
            arrive(got_x.at[o, dx], rx_r.at[o, dx])
            value += got_x[o, dx].astype(F32)
        if o:
            sum_z[o] = value.astype(BF)
            start(sum_z.at[o], got_z.at[o], rz_s.at[o], rz_r.at[o], (me.b, me.rep(dz=o)))
    for o in range(1, NZ):
        arrive(got_z.at[o], rz_r.at[o])
        value += got_z[o].astype(F32)

    load_cot.wait()
    agg = value.astype(BF)
    pre = jnp.dot(agg, weight[...], preferred_element_type=F32)
    sig = jax.nn.sigmoid(pre)
    dpre = (cot[...].astype(F32) * sig * (1.0 + pre * (1.0 - sig))).astype(BF)
    back[me.r] = lax.dot_general(
        dpre, weight[...], (((1,), (1,)), ((), ())), preferred_element_type=F32
    ).astype(BF)

    def over_x(o):
        slot = back.at[me.rep(dz=o)]
        start(slot, slot, gx_s.at[o, 1], gx_r.at[o, 1], (me.b, me.rep(dx=1)))
        start(slot, slot, gx_s.at[o, 3], gx_r.at[o, 3], (me.b, me.rep(dx=-1)))

    mine_back = back.at[me.r]
    for o in (1, 5, 2, 4, 3):
        start(mine_back, mine_back, gz_s.at[o], gz_r.at[o], (me.b, me.rep(dz=-o)))
        if o == 1:
            over_x(0)

    act_out[...] = (pre * sig).astype(BF)
    wsum[...] = lax.dot_general(agg, dpre, (((0,), (0,)), ((), ())), preferred_element_type=F32)
    half = SIDE
    w1_out[...] = wsum[pl.ds((1 - me.c) * half, half), :].astype(BF)
    start(w1_out, w1_in, wa_s.at[0], wa_r.at[0], sibling)
    back[PARTS] = jnp.zeros((SIDE, WIDTH), BF)

    def relay(o):
        near, onward = (1, 1) if o % 2 == 0 else (3, -1)
        slot = back.at[me.rep(dz=o, dx=-near)]
        arrive(slot, gx_r.at[o, near])
        start(slot, slot, gx_s.at[o, 2], gx_r.at[o, 2], (me.b, me.rep(dx=onward)))

    for o in (1, 5, 2, 4, 3):
        arrive(back.at[me.rep(dz=o)], gz_r.at[o])
        over_x(o)
        if o == 1:
            relay(0)
            arrive(w1_in, wa_r.at[0])
            w1 = wsum[pl.ds(me.c * half, half), :] + w1_in[...].astype(F32)
            wsum[0:half, :] = w1
            w2_out[...] = w1.astype(BF).reshape(NY, 16, WIDTH)
            for dy in range(1, NY):
                start(w2_out.at[lax.rem(me.y + dy, NY)], w2_in.at[dy], wy_s.at[dy], wy_r.at[dy],
                      (me.blk(dy=dy), me.r))
    for o in (1, 5, 2, 4, 3):
        relay(o)

    w2 = wsum[pl.ds(me.y * 16, 16), :]
    for dy in range(1, NY):
        arrive(w2_in.at[dy], wy_r.at[dy])
        w2 += w2_in[dy].astype(F32)
    w3_in[me.x] = w2.astype(BF)
    for dx in range(1, NX):
        slot = w3_in.at[me.x]
        start(slot, slot, wx_s.at[dx], wx_r.at[dx], (me.b, me.rep(dx=dx)))

    for o in range(NZ):
        far = (3 if o % 2 == 0 else 1)
        arrive(back.at[me.rep(dz=o, dx=-far)], gx_r.at[o, far])
        arrive(back.at[me.rep(dz=o, dx=2)], gx_r.at[o, 2])
    load_tiles.wait()

    def term(c):
        picked = jnp.concatenate([back[index[c * SLOTS + k]] for k in range(SLOTS)], axis=0)
        return lax.dot_general(
            tiles[c].reshape(SLOTS * SIDE, SIDE), picked, (((0,), (0,)), ((), ())),
            preferred_element_type=F32,
        )

    def to_sibling(p):
        return remote(to_core.at[p], from_core.at[p], core_s.at[p], core_r.at[p], sibling)

    def terms(p, carry):
        dy, e = group_of(p)
        y = lax.rem(me.y + dy + NY, NY)
        h = jnp.where(e == 1, 1 - me.h, me.h)
        base = (y * 2 + h) * 2
        to_core[p - 2] = term(base + 1 - me.c).astype(BF)
        to_sibling(p - 2).start()
        mine[p - 2] = term(base + me.c)
        return carry

    def ring(p):
        dy, e = GROUPS[p]
        to_sibling(p).wait_recv()
        value = mine[p] + from_core[p].astype(F32)
        for sign, step in ((1, up), (-1, down)):
            m = sign * dy
            if abs(dy) == 4:
                m = 4 if (sign > 0) == (e == 1) else 9
            elif dy and m < 0:
                continue
            k = HOPS.index((sign, e, m + 1)) if (sign, e, m + 1) in HOPS else None
            if k is not None:
                arrive(ring_in.at[k], ring_r.at[k])
                value += ring_in[k].astype(F32)
            if (sign, e, m) in HOPS:
                k = HOPS.index((sign, e, m))
                ring_out[k] = value.astype(BF)
                start(ring_out.at[k], ring_in.at[k], ring_s.at[k], ring_r.at[k], step)
        return value

    lax.fori_loop(2, 4, terms, 0)
    ring(0)
    ring(1)
    lax.fori_loop(4, 18, terms, 0)

    w3 = None
    for dx in range(1, NX):
        slot = w3_in.at[lax.rem(me.x + NX - dx, NX)]
        arrive(slot, wx_r.at[dx])
    w3 = sum((w3_in[i].astype(F32) for i in range(1, NX)), w3_in[0].astype(F32))
    zed = me.h * NZ + me.z
    w4_in[zed] = w3.astype(BF)
    for e in (0, 1):
        for dz in range(NZ):
            if e or dz:
                slot = w4_in.at[zed]
                start(slot, slot, wz_s.at[e, dz], wz_r.at[e, dz], (me.blk(e=e), me.rep(dz=dz)))

    for p in range(2, 10):
        ring(p)

    for e in (0, 1):
        for dz in range(NZ):
            if e or dz:
                h = 1 - me.h if e else me.h
                slot = w4_in.at[h * NZ + lax.rem(me.z + NZ - dz, NZ)]
                arrive(slot, wz_r.at[e, dz])
    w4 = sum((w4_in[i].astype(F32) for i in range(1, 2 * NZ)), w4_in[0].astype(F32))
    w5_in[me.y] = w4.astype(BF)

    for p in range(10, 14):
        ring(p)
    cross_out[...] = ring(14).astype(BF)
    start(cross_out, cross_in, cross_s.at[0], cross_r.at[0], other)
    for dy in range(1, NY):
        slot = w5_in.at[me.y]
        start(slot, slot, wo_s.at[dy], wo_r.at[dy], (me.blk(dy=dy), me.r))
    value = ring(15)
    for dy in range(1, NY):
        arrive(w5_in.at[lax.rem(me.y + NY - dy, NY)], wo_r.at[dy])
    start(w5_in, w6_in, wa_s.at[1], wa_r.at[1], sibling)
    weight_out[pl.ds(me.c * half, half), :] = w5_in[...].astype(F32).reshape(half, WIDTH)
    arrive(w6_in, wa_r.at[1])
    weight_out[pl.ds((1 - me.c) * half, half), :] = w6_in[...].astype(F32).reshape(half, WIDTH)
    arrive(cross_in, cross_r.at[0])
    grad_out[...] = (value + cross_in[...].astype(F32)).astype(BF)
    for copy in sends:
        copy.wait_send()

    def drain(p, carry):
        to_sibling(p).wait_send()
        return carry

    lax.fori_loop(0, 16, drain, 0)


def dma(*shape):
    return pltpu.SemaphoreType.DMA(shape)


def piece(*lead, dtype=BF):
    return pltpu.VMEM((*lead, SIDE, WIDTH), dtype)


def body(features, tiles, tile_rows, tile_count, weight, cotangent):
    slots = jnp.arange(SLOTS, dtype=jnp.int32)
    live = slots[None, :] < tile_count[0, :, 0][:, None]
    index = jnp.where(live, tile_rows[0, :, 0], PARTS).reshape(BLOCKS * SLOTS)

    gathered = pl.pallas_call(
        gather_kernel,
        out_shape=jax.ShapeDtypeStruct((BLOCKS, SIDE, WIDTH), BF),
        in_specs=[ANY],
        out_specs=VMEM,
        scratch_shapes=[dma(GATHER_SENDS), dma(BLOCKS), pltpu.SemaphoreType.DMA],
        compiler_params=pltpu.CompilerParams(
            collective_id=0, has_side_effects=True, vmem_limit_bytes=8 << 20
        ),
        name="gather_features",
    )(features)

    part = pl.pallas_call(
        forward_kernel,
        out_shape=jax.ShapeDtypeStruct((PARTS, SIDE, WIDTH), BF),
        in_specs=[SMEM, VMEM, VMEM],
        out_specs=VMEM,
        scratch_shapes=[piece(PARTS, dtype=F32)],
        compiler_params=pltpu.CompilerParams(vmem_limit_bytes=24 << 20),
        name="forward_tiles",
    )(index, tiles.reshape(BLOCKS, SLOTS, SIDE, SIDE), gathered)

    small = pltpu.VMEM((NY, 16, WIDTH), BF)
    activation, grad_rows, grad_weight = pl.pallas_call(
        back_kernel,
        out_shape=(
            jax.ShapeDtypeStruct((SIDE, WIDTH), BF),
            jax.ShapeDtypeStruct((SIDE, WIDTH), BF),
            jax.ShapeDtypeStruct((WIDTH, WIDTH), F32),
        ),
        in_specs=[SMEM, VMEM, ANY, VMEM, ANY],
        out_specs=(VMEM, VMEM, VMEM),
        scratch_shapes=[
            pltpu.VMEM((BLOCKS, SLOTS, SIDE, SIDE), BF),
            piece(),
            piece(NZ, NX), piece(NZ), piece(NZ),
            piece(PARTS + 1),
            piece(16), piece(16), piece(16, dtype=F32),
            piece(len(HOPS)), piece(len(HOPS)),
            piece(), piece(),
            pltpu.VMEM((WIDTH, WIDTH), F32),
            piece(), piece(),
            small, small,
            pltpu.VMEM((16, WIDTH), BF), pltpu.VMEM((NX, 16, WIDTH), BF),
            pltpu.VMEM((16, WIDTH), BF), pltpu.VMEM((2 * NZ, 16, WIDTH), BF),
            small, small,
            dma(3),
            dma(NZ, NX), dma(NZ, NX), dma(NZ), dma(NZ),
            dma(NZ), dma(NZ), dma(NZ, NX), dma(NZ, NX),
            dma(16), dma(16), dma(len(HOPS)), dma(len(HOPS)),
            dma(1), dma(1), dma(2), dma(2),
            dma(NY), dma(NY), dma(NX), dma(NX), dma(2, NZ), dma(2, NZ), dma(NY), dma(NY),
        ],
        compiler_params=pltpu.CompilerParams(
            collective_id=1, has_side_effects=True, vmem_limit_bytes=40 << 20
        ),
        name="aggregate_and_back",
    )(index, part, tiles, weight, cotangent)
    return activation, grad_rows, grad_weight


def solution(mesh):
    placed = (
        P("blk", None),
        P("blk", None, "rep", None, None, None),
        P("blk", None, "rep", None),
        P("blk", None, "rep"),
        P(),
        P("blk", None),
    )
    return jax.shard_map(
        body,
        mesh=mesh,
        in_specs=placed,
        out_specs=(P(("blk", "rep"), None), P(("blk", "rep"), None), P()),
        check_vma=False,
    )
```

```python
import jax
import jax.numpy as jnp
from jax import lax
from jax.experimental import pallas as pl
from jax.experimental.pallas import tpu as pltpu
from jax.sharding import PartitionSpec as P

NX, NY, NZ = 4, 8, 6
SIDE, WIDTH, PARTS, BLOCKS, SLOTS = 128, 256, 24, 32, 4
MESH = pl.DeviceIdType.MESH
BF, F32 = jnp.bfloat16, jnp.float32
VMEM = pl.BlockSpec(memory_space=pltpu.VMEM)
SMEM = pl.BlockSpec(memory_space=pltpu.SMEM)
ANY = pl.BlockSpec(memory_space=pl.ANY)


class Place:
    def __init__(self):
        self.b = lax.axis_index("blk")
        self.r = lax.axis_index("rep")
        self.y = lax.div(self.b, 4)
        self.h = lax.rem(lax.div(self.b, 2), 2)
        self.c = lax.rem(self.b, 2)
        self.z = lax.div(self.r, NX)
        self.x = lax.rem(self.r, NX)

    def blk(self, dy=0, e=0, flip=0):
        y = lax.rem(self.y + dy + NY, NY)
        h = 1 - self.h if e else self.h
        c = 1 - self.c if flip else self.c
        return (y * 2 + h) * 2 + c

    def rep(self, dz=0, dx=0):
        return lax.rem(self.z + dz + NZ, NZ) * NX + lax.rem(self.x + dx + NX, NX)


def greet(peers):
    barrier = pltpu.get_barrier_semaphore()
    for peer in peers:
        pl.semaphore_signal(barrier, inc=1, device_id=peer, device_id_type=MESH)
    pl.semaphore_wait(barrier, len(peers))


def remote(src, dst, send_sem, recv_sem, device):
    return pltpu.make_async_remote_copy(
        src_ref=src, dst_ref=dst, send_sem=send_sem, recv_sem=recv_sem,
        device_id=device, device_id_type=MESH,
    )


NEAR = [sorted((z for z in range(NZ) if z != home), key=lambda z: abs(z - home)) for home in range(NZ)]
HOPS = [(e, dy) for dy in (4, 3, -3, 2, -2, 1, -1) for e in (1, 0)]
GROUPS = [(1, 4), (0, 4)] + [(e, s * m) for m in (3, 2, 1) for s in (1, -1) for e in (1, 0)] + [(1, 0), (0, 0)]


def choose(at, values):
    out = values[0]
    for i, value in enumerate(values[1:], 1):
        out = jnp.where(at == i, value, out)
    return out


def layer_kernel(
    rows, counts, feat, tiles_hbm, weight, cot_hbm,
    act_out, grad_out, weight_out,
    feats, tiles, tiles_t, prods, sums, part, marks, marks_s, cot,
    got_x, mid_x, sum_z, got_z, back, to_core, from_core, mine, ring_out, ring_in,
    cross_out, cross_in, wsum, w1_out, w1_in, w2_out, w2_in, w3_in, w4_in, w5_in, w6_in,
    local_sem, feat_s, feat_r, rx_s, rx_r, rz_s, rz_r, gz_s, gz_r, gx_s, gx_r, core_s, core_r, ring_s, ring_r,
    cross_s, cross_r, wa_s, wa_r, wy_s, wy_r, wx_s, wx_r, wz_s, wz_r, wo_s, wo_r,
):
    me = Place()
    sibling = (me.blk(flip=1), me.r)
    other = (me.blk(e=1), me.r)
    far = me.rep(dz=3)
    peers = [sibling]
    peers += [(me.blk(dy=dy), me.r) for dy in range(1, NY)]
    peers += [(me.b, me.rep(dx=dx)) for dx in range(1, NX)]
    peers += [(me.blk(e=e), me.rep(dz=dz)) for e in (0, 1) for dz in range(NZ) if e or dz]

    load_tiles = pltpu.make_async_copy(tiles_hbm.at[0, :, 0], tiles, local_sem.at[0])
    load_tiles.start()
    load_cot = pltpu.make_async_copy(cot_hbm.at[pl.ds(me.r * SIDE, SIDE), :], cot, local_sem.at[1])
    load_cot.start()
    own = feat.at[pl.ds(me.r * SIDE, SIDE), :]
    load_own = pltpu.make_async_copy(own, feats.at[me.b], local_sem.at[2])
    load_own.start()
    greet(peers)
    sends = []

    def start(*args):
        copy = remote(*args)
        copy.start()
        sends.append(copy)

    def arrive(dst, sem):
        remote(dst, dst, local_sem.at[3], sem, sibling).wait_recv()

    def feat_send(src, slot, lane, device):
        start(src, feats.at[slot], feat_s.at[lane, slot], feat_r.at[slot], device)

    def feat_arrive(slot):
        arrive(feats.at[slot], feat_r.at[slot])

    def feat_spread(src, slot):
        for n, dy in enumerate((2, -2, 1, -1)):
            feat_send(src, slot, n, (me.blk(dy=dy), me.r))
        feat_send(src, slot, 4, sibling)

    feat_send(feat.at[pl.ds(far * SIDE, SIDE), :], me.b, 5, (me.blk(e=1), far))
    feat_spread(own, me.b)

    lane = lax.broadcasted_iota(jnp.int32, (8, SIDE), 1)
    nought = jnp.zeros((8, SIDE), jnp.int32)

    def target(c, k):
        return jnp.where(k < counts[c], rows[k, c], PARTS)

    def slot_key(s):
        return target(lax.div(s, SLOTS), lax.rem(s, SLOTS))

    def spread(s, carry):
        unique, below, upto = carry
        key = slot_key(s)
        unique = jnp.where(lane == s, key * SIDE + s, unique)
        below += jnp.where(lane > key, 1, 0)
        upto += jnp.where(lane >= key, 1, 0)
        return unique, below, upto

    def rank_of(s, rank):
        return rank + jnp.where(unique > slot_key(s) * SIDE + s, 1, 0)

    def place(s, carry):
        order, keys = carry
        hit = lane == marks_s[0, 0, s]
        return jnp.where(hit, s, order), jnp.where(hit, slot_key(s), keys)

    sums[SIDE] = jnp.zeros((SIDE, WIDTH), BF)
    back[PARTS] = jnp.zeros((SIDE, WIDTH), BF)

    def turn(lo, hi):
        def body(c, carry):
            tiles_t[c] = tiles[c].reshape(SLOTS * SIDE, SIDE).T
            return carry

        lax.fori_loop(lo, hi, body, 0)

    def column(c):
        value = jnp.dot(tiles[c].reshape(SLOTS * SIDE, SIDE), feats[c], preferred_element_type=F32)
        prods[pl.ds(c * SLOTS, SLOTS)] = value.reshape(SLOTS, SIDE, WIDTH)

    def columns(which, flip):
        def body(j, carry):
            e, dy = (choose(j, v) for v in zip(*which))
            y = lax.rem(me.y + dy + NY, NY)
            h = jnp.where(e == 1, 1 - me.h, me.h)
            c = (y * 2 + h) * 2 + (1 - me.c if flip else me.c)
            if flip:
                feat_arrive(c)
            column(c)
            return carry

        lax.fori_loop(0, len(which), body, 0)

    def onward(e):
        for dy in (-2, 2):
            slot = me.blk(dy=dy, e=e)
            feat_arrive(slot)
            if (dy < 0) == (e == 1):
                feat_send(feats.at[slot], slot, 1 if dy > 0 else 0, (me.blk(dy=-dy), me.r))
            step = -1 if dy > 0 else 1
            feat_send(feats.at[slot], slot, 2, (me.blk(dy=step), me.r))
            feat_send(feats.at[slot], slot, 4, sibling)

    def settle(e, *dys):
        for dy in dys:
            slot = me.blk(dy=dy, e=e)
            feat_arrive(slot)
            feat_send(feats.at[slot], slot, 4, sibling)

    unique, below, upto = lax.fori_loop(0, SIDE, spread, (nought, nought, nought), unroll=8)
    onward(0)
    crossed = me.blk(e=1)
    feat_arrive(crossed)
    feat_spread(feats.at[crossed], crossed)
    settle(0, 1, -1)
    marks[0] = lax.fori_loop(0, SIDE, rank_of, nought, unroll=8)
    marks[3] = jnp.where(upto > below, upto - 1, SIDE)
    pltpu.sync_copy(marks.at[0], marks_s.at[0])
    onward(1)
    settle(1, 1, -1)
    settle(0, 3, -3, 4)
    order, keys = lax.fori_loop(0, SIDE, place, (nought, nought), unroll=8)
    marks[1] = order
    marks[2] = keys
    pltpu.sync_copy(marks.at[pl.ds(1, 3)], marks_s.at[pl.ds(1, 3)])
    load_tiles.wait()
    load_own.wait()
    early = [(0, 0), (1, 0)] + [(0, dy) for dy in (1, -1, 2, -2)] + [(1, dy) for dy in (1, -1, 2, -2)]
    late = [(0, 3), (0, -3), (0, 4), (1, 3), (1, -3), (1, 4)]
    columns(early + late[:3], 0)
    settle(1, 3, -3, 4)
    columns(early, 1)
    columns(late[3:], 0)
    columns(late, 1)

    for lo in range(0, SIDE, 64):
        span = slice(lo, lo + 64)

        def scan(p, total):
            key = marks_s[2, 0, p]
            before = marks_s[2, 0, jnp.maximum(p - 1, 0)]
            keep = jnp.where(key == before, 1.0, 0.0).astype(F32)
            total = total * keep + prods[marks_s[1, 0, p], span, :]
            sums[p, span, :] = total.astype(BF)
            return total

        lax.fori_loop(0, SIDE, scan, jnp.zeros((64, WIDTH), F32), unroll=4)

    def pick(t):
        part[t] = sums[marks_s[3, 0, t]]

    at_z = [choose(me.z, [NEAR[home][NZ - 2 - k] for home in range(NZ)]) for k in range(NZ - 1)] + [me.z]

    def tile_at(k, dx=0):
        return at_z[k] * NX + lax.rem(me.x + dx + NX, NX)

    def ways(k):
        return 1 if k % 2 == 0 else -1

    def toward(dx):
        return (me.b, me.rep(dx=dx))

    for k in range(NZ):
        pick(tile_at(k, 2))
        start(part.at[tile_at(k, 2)], got_x.at[k, 0], rx_s.at[k, 0], rx_r.at[k, 0], toward(ways(k)))
    for k in range(NZ):
        for dx in (0, 1, -1):
            pick(tile_at(k, dx))

    def pass_on(k):
        arrive(got_x.at[k, 0], rx_r.at[k, 0])
        mid_x[k] = (got_x[k, 0].astype(F32) + part[tile_at(k, ways(k))].astype(F32)).astype(BF)
        start(mid_x.at[k], got_x.at[k, 1], rx_s.at[k, 1], rx_r.at[k, 1], toward(ways(k)))
        start(part.at[tile_at(k, -ways(k))], got_x.at[k, 2], rx_s.at[k, 2], rx_r.at[k, 2],
              toward(-ways(k)))

    def sum_x(k):
        arrive(got_x.at[k, 1], rx_r.at[k, 1])
        arrive(got_x.at[k, 2], rx_r.at[k, 2])
        value = part[tile_at(k)].astype(F32) + got_x[k, 1].astype(F32) + got_x[k, 2].astype(F32)
        if k < NZ - 1:
            sum_z[k] = value.astype(BF)
            slot = lax.rem(me.z - at_z[k] + NZ, NZ)
            start(sum_z.at[k], got_z.at[slot], rz_s.at[k], rz_r.at[slot], (me.b, at_z[k] * NX + me.x))
        return value

    for i in range(NZ + 2):
        if i < NZ:
            pass_on(i)
        if i >= 2:
            value = sum_x(i - 2)
    turn(0, BLOCKS // 2)
    for o in range(1, NZ):
        arrive(got_z.at[o], rz_r.at[o])
        value += got_z[o].astype(F32)

    load_cot.wait()
    agg = value.astype(BF)
    pre = jnp.dot(agg, weight[...], preferred_element_type=F32)
    sig = jax.nn.sigmoid(pre)
    dpre = (cot[...].astype(F32) * sig * (1.0 + pre * (1.0 - sig))).astype(BF)
    back[me.r] = lax.dot_general(
        dpre, weight[...], (((1,), (1,)), ((), ())), preferred_element_type=F32
    ).astype(BF)

    at_z.reverse()

    def over_x(k):
        slot = back.at[tile_at(k)]
        for dx in (1, -1):
            start(slot, slot, gx_s.at[k, dx % NX], gx_r.at[k, dx % NX], toward(dx))

    def relay(k):
        way = ways(k)
        slot = back.at[tile_at(k, -way)]
        arrive(slot, gx_r.at[k, way % NX])
        start(slot, slot, gx_s.at[k, 2], gx_r.at[k, 2], toward(way))

    mine_back = back.at[me.r]
    over_x(0)
    for k in range(1, NZ):
        start(mine_back, mine_back, gz_s.at[k], gz_r.at[me.z], (me.b, at_z[k] * NX + me.x))

    act_out[...] = (pre * sig).astype(BF)
    wsum[...] = lax.dot_general(agg, dpre, (((0,), (0,)), ((), ())), preferred_element_type=F32)
    half = SIDE
    w1_out[...] = wsum[pl.ds((1 - me.c) * half, half), :].astype(BF)
    start(w1_out, w1_in, wa_s.at[0], wa_r.at[0], sibling)

    def from_z(k):
        arrive(back.at[tile_at(k)], gz_r.at[at_z[k]])
        over_x(k)

    from_z(1)
    relay(0)
    from_z(2)
    arrive(w1_in, wa_r.at[0])
    w1 = wsum[pl.ds(me.c * half, half), :] + w1_in[...].astype(F32)
    wsum[0:half, :] = w1
    w2_out[...] = w1.astype(BF).reshape(NY, 16, WIDTH)
    for dy in range(1, NY):
        start(w2_out.at[lax.rem(me.y + dy, NY)], w2_in.at[dy], wy_s.at[dy], wy_r.at[dy],
              (me.blk(dy=dy), me.r))
    turn(BLOCKS // 2, 3 * BLOCKS // 4)
    for k in range(3, NZ):
        from_z(k)
        relay(k - 2)
    relay(NZ - 2)
    turn(3 * BLOCKS // 4, BLOCKS)
    relay(NZ - 1)

    w2 = wsum[pl.ds(me.y * 16, 16), :]
    for dy in range(1, NY):
        arrive(w2_in.at[dy], wy_r.at[dy])
        w2 += w2_in[dy].astype(F32)
    w3_in[me.x] = w2.astype(BF)
    for dx in range(1, NX):
        slot = w3_in.at[me.x]
        start(slot, slot, wx_s.at[dx], wx_r.at[dx], (me.b, me.rep(dx=dx)))

    for k in range(NZ):
        arrive(back.at[tile_at(k, ways(k))], gx_r.at[k, -ways(k) % NX])
        arrive(back.at[tile_at(k, 2)], gx_r.at[k, 2])

    def term(c):
        picked = jnp.concatenate([back[target(c, k)] for k in range(SLOTS)], axis=0)
        return jnp.dot(tiles_t[c], picked, preferred_element_type=F32)

    def to_sibling(p):
        return remote(to_core.at[p], from_core.at[p], core_s.at[p], core_r.at[p], sibling)

    def terms(p, carry):
        e, dy = (choose(p, v) for v in zip(*GROUPS))
        y = lax.rem(me.y + dy + NY, NY)
        h = jnp.where(e == 1, 1 - me.h, me.h)
        base = (y * 2 + h) * 2
        to_core[p] = term(base + 1 - me.c).astype(BF)
        to_sibling(p).start()
        mine[p] = term(base + me.c)
        return carry

    def both(e, dy):
        p = GROUPS.index((e, dy))
        to_sibling(p).wait_recv()
        return mine[p] + from_core[p].astype(F32)

    def hop(e, dy, value):
        k = HOPS.index((e, dy))
        ring_out[k] = value.astype(BF)
        step = dy if abs(dy) < 3 else (dy - 2 if dy > 0 else dy + 2)
        if dy == 4 and e == 0:
            step = -2
        start(ring_out.at[k], ring_in.at[k], ring_s.at[k], ring_r.at[k], (me.blk(dy=step), me.r))

    def landed(e, dy):
        k = HOPS.index((e, dy))
        arrive(ring_in.at[k], ring_r.at[k])
        return ring_in[k].astype(F32)

    def far_hops(e):
        for sign in (1, -1):
            value = both(e, 2 * sign) + landed(e, 3 * sign)
            if (sign > 0) == (e == 1):
                value += landed(e, 4)
            hop(e, 2 * sign, value)

    def owned(e):
        value = both(e, 0)
        for dy in (1, -1, 2, -2):
            value += landed(e, dy)
        return value

    lax.fori_loop(0, 6, terms, 0)
    for e, dy in GROUPS[:6]:
        hop(e, dy, both(e, dy))
    lax.fori_loop(6, 16, terms, 0)

    w3 = None
    for dx in range(1, NX):
        slot = w3_in.at[lax.rem(me.x + NX - dx, NX)]
        arrive(slot, wx_r.at[dx])
    w3 = sum((w3_in[i].astype(F32) for i in range(1, NX)), w3_in[0].astype(F32))
    zed = me.h * NZ + me.z
    w4_in[zed] = w3.astype(BF)
    for e in (0, 1):
        for dz in range(NZ):
            if e or dz:
                slot = w4_in.at[zed]
                start(slot, slot, wz_s.at[e, dz], wz_r.at[e, dz], (me.blk(e=e), me.rep(dz=dz)))

    far_hops(1)
    for dy in (1, -1):
        hop(1, dy, both(1, dy))
    far_hops(0)
    for dy in (1, -1):
        hop(0, dy, both(0, dy))

    for e in (0, 1):
        for dz in range(NZ):
            if e or dz:
                h = 1 - me.h if e else me.h
                slot = w4_in.at[h * NZ + lax.rem(me.z + NZ - dz, NZ)]
                arrive(slot, wz_r.at[e, dz])
    w4 = sum((w4_in[i].astype(F32) for i in range(1, 2 * NZ)), w4_in[0].astype(F32))
    w5_in[me.y] = w4.astype(BF)

    cross_out[...] = owned(1).astype(BF)
    start(cross_out, cross_in, cross_s.at[0], cross_r.at[0], other)
    for dy in range(1, NY):
        slot = w5_in.at[me.y]
        start(slot, slot, wo_s.at[dy], wo_r.at[dy], (me.blk(dy=dy), me.r))
    value = owned(0)
    for dy in range(1, NY):
        arrive(w5_in.at[lax.rem(me.y + NY - dy, NY)], wo_r.at[dy])
    start(w5_in, w6_in, wa_s.at[1], wa_r.at[1], sibling)
    weight_out[pl.ds(me.c * half, half), :] = w5_in[...].astype(F32).reshape(half, WIDTH)
    arrive(w6_in, wa_r.at[1])
    weight_out[pl.ds((1 - me.c) * half, half), :] = w6_in[...].astype(F32).reshape(half, WIDTH)
    arrive(cross_in, cross_r.at[0])
    grad_out[...] = (value + cross_in[...].astype(F32)).astype(BF)
    for copy in sends:
        copy.wait_send()

    def drain(p, carry):
        to_sibling(p).wait_send()
        return carry

    lax.fori_loop(0, 16, drain, 0)


def dma(*shape):
    return pltpu.SemaphoreType.DMA(shape)


def piece(*lead, dtype=BF):
    return pltpu.VMEM((*lead, SIDE, WIDTH), dtype)


def body(features, tiles, tile_rows, tile_count, weight, cotangent):
    small = pltpu.VMEM((NY, 16, WIDTH), BF)
    return pl.pallas_call(
        layer_kernel,
        out_shape=(
            jax.ShapeDtypeStruct((SIDE, WIDTH), BF),
            jax.ShapeDtypeStruct((SIDE, WIDTH), BF),
            jax.ShapeDtypeStruct((WIDTH, WIDTH), F32),
        ),
        in_specs=[SMEM, SMEM, ANY, ANY, VMEM, ANY],
        out_specs=(VMEM, VMEM, VMEM),
        scratch_shapes=[
            piece(BLOCKS),
            pltpu.VMEM((BLOCKS, SLOTS, SIDE, SIDE), BF),
            pltpu.VMEM((BLOCKS, SIDE, SLOTS * SIDE), BF),
            piece(BLOCKS * SLOTS, dtype=F32),
            piece(BLOCKS * SLOTS + 1),
            piece(PARTS),
            pltpu.VMEM((4, 8, SIDE), jnp.int32),
            pltpu.SMEM((4, 8, SIDE), jnp.int32),
            piece(),
            piece(NZ, 3), piece(NZ), piece(NZ), piece(NZ),
            piece(PARTS + 1),
            piece(16), piece(16), piece(16, dtype=F32),
            piece(len(HOPS)), piece(len(HOPS)),
            piece(), piece(),
            pltpu.VMEM((WIDTH, WIDTH), F32),
            piece(), piece(),
            small, small,
            pltpu.VMEM((NX, 16, WIDTH), BF),
            pltpu.VMEM((2 * NZ, 16, WIDTH), BF),
            small, small,
            dma(4), dma(6, BLOCKS), dma(BLOCKS),
            dma(NZ, 3), dma(NZ, 3), dma(NZ), dma(NZ),
            dma(NZ), dma(NZ), dma(NZ, NX), dma(NZ, NX),
            dma(16), dma(16), dma(len(HOPS)), dma(len(HOPS)),
            dma(1), dma(1), dma(2), dma(2),
            dma(NY), dma(NY), dma(NX), dma(NX), dma(2, NZ), dma(2, NZ), dma(NY), dma(NY),
        ],
        compiler_params=pltpu.CompilerParams(
            collective_id=0, has_side_effects=True, vmem_limit_bytes=58 << 20
        ),
        name="graph_layer",
    )(tile_rows[0, :, 0].T, tile_count[0, :, 0], features, tiles, weight, cotangent)


def solution(mesh):
    placed = (
        P("blk", None),
        P("blk", None, "rep", None, None, None),
        P("blk", None, "rep", None),
        P("blk", None, "rep"),
        P(),
        P("blk", None),
    )
    return jax.shard_map(
        body,
        mesh=mesh,
        in_specs=placed,
        out_specs=(P(("blk", "rep"), None), P(("blk", "rep"), None), P()),
        check_vma=False,
    )
```

```python
import jax
import jax.numpy as jnp
from jax import lax
from jax.experimental import pallas as pl
from jax.experimental.pallas import tpu as pltpu
from jax.sharding import PartitionSpec as P

NX, NY, NZ = 4, 8, 6
SIDE, WIDTH, PARTS, BLOCKS, SLOTS = 128, 256, 24, 32, 4
MESH = pl.DeviceIdType.MESH
BF, F32 = jnp.bfloat16, jnp.float32
VMEM = pl.BlockSpec(memory_space=pltpu.VMEM)
SMEM = pl.BlockSpec(memory_space=pltpu.SMEM)
ANY = pl.BlockSpec(memory_space=pl.ANY)


class Place:
    def __init__(self):
        self.b = lax.axis_index("blk")
        self.r = lax.axis_index("rep")
        self.y = lax.div(self.b, 4)
        self.h = lax.rem(lax.div(self.b, 2), 2)
        self.c = lax.rem(self.b, 2)
        self.z = lax.div(self.r, NX)
        self.x = lax.rem(self.r, NX)

    def blk(self, dy=0, e=0, flip=0):
        y = lax.rem(self.y + dy + NY, NY)
        h = 1 - self.h if e else self.h
        c = 1 - self.c if flip else self.c
        return (y * 2 + h) * 2 + c

    def rep(self, dz=0, dx=0):
        return lax.rem(self.z + dz + NZ, NZ) * NX + lax.rem(self.x + dx + NX, NX)


def greet(peers):
    barrier = pltpu.get_barrier_semaphore()
    for peer in peers:
        pl.semaphore_signal(barrier, inc=1, device_id=peer, device_id_type=MESH)
    pl.semaphore_wait(barrier, len(peers))


def remote(src, dst, send_sem, recv_sem, device):
    return pltpu.make_async_remote_copy(
        src_ref=src, dst_ref=dst, send_sem=send_sem, recv_sem=recv_sem,
        device_id=device, device_id_type=MESH,
    )


HOPS = [(e, dy) for dy in (4, 3, -3, 2, -2, 1, -1) for e in (1, 0)]
GROUPS = [(1, 4), (0, 4)] + [(e, s * m) for m in (3, 2, 1) for s in (1, -1) for e in (1, 0)] + [(1, 0), (0, 0)]


def choose(at, values):
    out = values[0]
    for i, value in enumerate(values[1:], 1):
        out = jnp.where(at == i, value, out)
    return out


def layer_kernel(
    rows, counts, feat, tiles_hbm, weight, cot_hbm,
    act_out, grad_out, weight_out,
    feats, tiles, tiles_t, prods, sums, part, marks, marks_s, cot,
    got_x, mid_x, sum_z, got_z, back, to_core, from_core, mine, ring_out, ring_in,
    cross_out, cross_in, wsum, w1_out, w1_in, w2_out, w2_in, w3_in, w4_in, w5_in, w6_in,
    local_sem, feat_s, feat_r, rx_s, rx_r, rz_s, rz_r, gz_s, gz_r, gx_s, gx_r, core_s, core_r, ring_s, ring_r,
    cross_s, cross_r, wa_s, wa_r, wy_s, wy_r, wx_s, wx_r, wz_s, wz_r, wo_s, wo_r,
):
    me = Place()
    sibling = (me.blk(flip=1), me.r)
    other = (me.blk(e=1), me.r)
    far = me.rep(dz=3)
    peers = [sibling]
    peers += [(me.blk(dy=dy), me.r) for dy in range(1, NY)]
    peers += [(me.b, me.rep(dx=dx)) for dx in range(1, NX)]
    peers += [(me.blk(e=e), me.rep(dz=dz)) for e in (0, 1) for dz in range(NZ) if e or dz]

    load_tiles = pltpu.make_async_copy(tiles_hbm.at[0, :, 0], tiles, local_sem.at[0])
    load_tiles.start()
    load_cot = pltpu.make_async_copy(cot_hbm.at[pl.ds(me.r * SIDE, SIDE), :], cot, local_sem.at[1])
    load_cot.start()
    own = feat.at[pl.ds(me.r * SIDE, SIDE), :]
    load_own = pltpu.make_async_copy(own, feats.at[me.b], local_sem.at[2])
    load_own.start()
    greet(peers)
    sends = []

    def start(*args):
        copy = remote(*args)
        copy.start()
        sends.append(copy)

    def arrive(dst, sem):
        remote(dst, dst, local_sem.at[3], sem, sibling).wait_recv()

    def feat_send(src, slot, lane, device):
        start(src, feats.at[slot], feat_s.at[lane, slot], feat_r.at[slot], device)

    def feat_arrive(slot):
        arrive(feats.at[slot], feat_r.at[slot])

    def feat_spread(src, slot):
        for n, dy in enumerate((2, -2, 1, -1)):
            feat_send(src, slot, n, (me.blk(dy=dy), me.r))
        feat_send(src, slot, 4, sibling)

    feat_send(feat.at[pl.ds(far * SIDE, SIDE), :], me.b, 5, (me.blk(e=1), far))
    feat_spread(own, me.b)

    lane = lax.broadcasted_iota(jnp.int32, (8, SIDE), 1)
    nought = jnp.zeros((8, SIDE), jnp.int32)

    def target(c, k):
        return jnp.where(k < counts[c], rows[k, c], PARTS)

    def slot_key(s):
        return target(lax.div(s, SLOTS), lax.rem(s, SLOTS))

    def spread(s, carry):
        unique, below, upto = carry
        key = slot_key(s)
        unique = jnp.where(lane == s, key * SIDE + s, unique)
        below += jnp.where(lane > key, 1, 0)
        upto += jnp.where(lane >= key, 1, 0)
        return unique, below, upto

    def rank_of(s, rank):
        return rank + jnp.where(unique > slot_key(s) * SIDE + s, 1, 0)

    def place(s, carry):
        order, keys = carry
        hit = lane == marks_s[0, 0, s]
        return jnp.where(hit, s, order), jnp.where(hit, slot_key(s), keys)

    sums[SIDE] = jnp.zeros((SIDE, WIDTH), BF)
    back[PARTS] = jnp.zeros((SIDE, WIDTH), BF)

    def turn(lo, hi):
        def body(c, carry):
            tiles_t[c] = tiles[c].reshape(SLOTS * SIDE, SIDE).T
            return carry

        lax.fori_loop(lo, hi, body, 0)

    def column(c):
        value = jnp.dot(tiles[c].reshape(SLOTS * SIDE, SIDE), feats[c], preferred_element_type=F32)
        prods[pl.ds(c * SLOTS, SLOTS)] = value.reshape(SLOTS, SIDE, WIDTH)

    def columns(which, flip):
        def body(j, carry):
            e, dy = (choose(j, v) for v in zip(*which))
            y = lax.rem(me.y + dy + NY, NY)
            h = jnp.where(e == 1, 1 - me.h, me.h)
            c = (y * 2 + h) * 2 + (1 - me.c if flip else me.c)
            if flip:
                feat_arrive(c)
            column(c)
            return carry

        lax.fori_loop(0, len(which), body, 0, unroll=2)

    def onward(e):
        for dy in (-2, 2):
            slot = me.blk(dy=dy, e=e)
            feat_arrive(slot)
            if (dy < 0) == (e == 1):
                feat_send(feats.at[slot], slot, 1 if dy > 0 else 0, (me.blk(dy=-dy), me.r))
            step = -1 if dy > 0 else 1
            feat_send(feats.at[slot], slot, 2, (me.blk(dy=step), me.r))
            feat_send(feats.at[slot], slot, 4, sibling)

    def settle(e, *dys):
        for dy in dys:
            slot = me.blk(dy=dy, e=e)
            feat_arrive(slot)
            feat_send(feats.at[slot], slot, 4, sibling)

    unique, below, upto = lax.fori_loop(0, SIDE, spread, (nought, nought, nought), unroll=8)
    onward(0)
    crossed = me.blk(e=1)
    feat_arrive(crossed)
    feat_spread(feats.at[crossed], crossed)
    settle(0, 1, -1)
    marks[0] = lax.fori_loop(0, SIDE, rank_of, nought, unroll=8)
    marks[3] = jnp.where(upto > below, upto - 1, SIDE)
    pltpu.sync_copy(marks.at[0], marks_s.at[0])
    onward(1)
    settle(1, 1, -1)
    settle(0, 3, -3, 4)
    order, keys = lax.fori_loop(0, SIDE, place, (nought, nought), unroll=8)
    marks[1] = order
    marks[2] = keys
    pltpu.sync_copy(marks.at[pl.ds(1, 3)], marks_s.at[pl.ds(1, 3)])
    load_tiles.wait()
    load_own.wait()
    early = [(0, 0), (1, 0)] + [(0, dy) for dy in (1, -1, 2, -2)] + [(1, dy) for dy in (1, -1, 2, -2)]
    late = [(0, 3), (0, -3), (0, 4), (1, 3), (1, -3), (1, 4)]
    columns(early + late[:3], 0)
    columns(early, 1)
    settle(1, 3, -3, 4)
    columns(late[3:], 0)
    columns(late, 1)

    for lo in range(0, SIDE, 64):
        span = slice(lo, lo + 64)

        def scan(p, total):
            key = marks_s[2, 0, p]
            before = marks_s[2, 0, jnp.maximum(p - 1, 0)]
            keep = jnp.where(key == before, 1.0, 0.0).astype(F32)
            total = total * keep + prods[marks_s[1, 0, p], span, :]
            sums[p, span, :] = total.astype(BF)
            return total

        lax.fori_loop(0, SIDE, scan, jnp.zeros((64, WIDTH), F32), unroll=4)

    def pick(t):
        part[t] = sums[marks_s[3, 0, t]]

    run, spot = lax.div(me.z, 3), lax.rem(me.z, 3)

    def place_z(j, across):
        return (1 - run if across else run) * 3 + lax.rem(spot + j, 3)

    at_z = [place_z(1, 1), place_z(2, 1), place_z(0, 1), place_z(1, 0), place_z(2, 0), me.z]

    def along(z):
        return (me.b, z * NX + me.x)

    def tile_at(k, dx=0):
        return at_z[k] * NX + lax.rem(me.x + dx + NX, NX)

    def ways(k):
        return 1 if k % 2 == 0 else -1

    def toward(dx):
        return (me.b, me.rep(dx=dx))

    for k in range(NZ):
        pick(tile_at(k, 2))
        start(part.at[tile_at(k, 2)], got_x.at[k, 0], rx_s.at[k, 0], rx_r.at[k, 0], toward(ways(k)))
    for k in range(NZ):
        for dx in (0, 1, -1):
            pick(tile_at(k, dx))

    def pass_on(k):
        arrive(got_x.at[k, 0], rx_r.at[k, 0])
        mid_x[k] = (got_x[k, 0].astype(F32) + part[tile_at(k, ways(k))].astype(F32)).astype(BF)
        start(mid_x.at[k], got_x.at[k, 1], rx_s.at[k, 1], rx_r.at[k, 1], toward(ways(k)))
        start(part.at[tile_at(k, -ways(k))], got_x.at[k, 2], rx_s.at[k, 2], rx_r.at[k, 2],
              toward(-ways(k)))

    def sum_x(k):
        arrive(got_x.at[k, 1], rx_r.at[k, 1])
        arrive(got_x.at[k, 2], rx_r.at[k, 2])
        value = part[tile_at(k)].astype(F32) + got_x[k, 1].astype(F32) + got_x[k, 2].astype(F32)
        if k in (0, 1, 3, 4):
            z_send(k, value, place_z(k % 3 + 1, 0))
        return value

    def z_send(k, value, z):
        sum_z[k] = value.astype(BF)
        start(sum_z.at[k], got_z.at[k], rz_s.at[k], rz_r.at[k], along(z))

    def z_got(k):
        arrive(got_z.at[k], rz_r.at[k])
        return got_z[k].astype(F32)

    totals = {}
    for i in range(NZ + 2):
        if i < NZ:
            pass_on(i)
        if i >= 2:
            totals[i - 2] = sum_x(i - 2)
        if i == 5:
            z_send(2, totals[2] + z_got(0) + z_got(1), place_z(0, 1))
    turn(0, BLOCKS // 2)
    value = totals[NZ - 1]
    for k in (3, 4, 2):
        value += z_got(k)

    load_cot.wait()
    agg = value.astype(BF)
    pre = jnp.dot(agg, weight[...], preferred_element_type=F32)
    sig = jax.nn.sigmoid(pre)
    dpre = (cot[...].astype(F32) * sig * (1.0 + pre * (1.0 - sig))).astype(BF)
    back[me.r] = lax.dot_general(
        dpre, weight[...], (((1,), (1,)), ((), ())), preferred_element_type=F32
    ).astype(BF)

    at_z = [me.z, place_z(1, 0), place_z(2, 0), place_z(0, 1), place_z(1, 1), place_z(2, 1)]

    def over_x(k):
        slot = back.at[tile_at(k)]
        for dx in (1, -1):
            start(slot, slot, gx_s.at[k, dx % NX], gx_r.at[k, dx % NX], toward(dx))

    def relay(k):
        way = ways(k)
        slot = back.at[tile_at(k, -way)]
        arrive(slot, gx_r.at[k, way % NX])
        start(slot, slot, gx_s.at[k, 2], gx_r.at[k, 2], toward(way))

    mine_back = back.at[me.r]
    for k in (3, 2, 1):
        start(mine_back, mine_back, gz_s.at[k], gz_r.at[me.z], along(at_z[k]))
    over_x(0)

    act_out[...] = (pre * sig).astype(BF)
    wsum[...] = lax.dot_general(agg, dpre, (((0,), (0,)), ((), ())), preferred_element_type=F32)
    half = SIDE
    w1_out[...] = wsum[pl.ds((1 - me.c) * half, half), :].astype(BF)
    start(w1_out, w1_in, wa_s.at[0], wa_r.at[0], sibling)

    def from_z(k):
        slot = back.at[tile_at(k)]
        arrive(slot, gz_r.at[at_z[k]])
        if k == 3:
            for j in (2, 1):
                start(slot, slot, gz_s.at[3 + j], gz_r.at[at_z[k]], along(at_z[j]))
        over_x(k)

    for k in (3, 1, 2):
        from_z(k)
    relay(0)
    arrive(w1_in, wa_r.at[0])
    w1 = wsum[pl.ds(me.c * half, half), :] + w1_in[...].astype(F32)
    wsum[0:half, :] = w1
    w2_out[...] = w1.astype(BF).reshape(NY, 16, WIDTH)
    for dy in range(1, NY):
        start(w2_out.at[lax.rem(me.y + dy, NY)], w2_in.at[dy], wy_s.at[dy], wy_r.at[dy],
              (me.blk(dy=dy), me.r))
    turn(BLOCKS // 2, 3 * BLOCKS // 4)
    for k in (4, 5):
        from_z(k)
    for k in (1, 2, 3):
        relay(k)
    turn(3 * BLOCKS // 4, BLOCKS)
    for k in (4, 5):
        relay(k)

    w2 = wsum[pl.ds(me.y * 16, 16), :]
    for dy in range(1, NY):
        arrive(w2_in.at[dy], wy_r.at[dy])
        w2 += w2_in[dy].astype(F32)
    w3_in[me.x] = w2.astype(BF)
    for dx in range(1, NX):
        slot = w3_in.at[me.x]
        start(slot, slot, wx_s.at[dx], wx_r.at[dx], (me.b, me.rep(dx=dx)))

    for k in range(NZ):
        arrive(back.at[tile_at(k, ways(k))], gx_r.at[k, -ways(k) % NX])
        arrive(back.at[tile_at(k, 2)], gx_r.at[k, 2])

    def term(c):
        picked = jnp.concatenate([back[target(c, k)] for k in range(SLOTS)], axis=0)
        return jnp.dot(tiles_t[c], picked, preferred_element_type=F32)

    def to_sibling(p):
        return remote(to_core.at[p], from_core.at[p], core_s.at[p], core_r.at[p], sibling)

    def terms(p, carry):
        e, dy = (choose(p, v) for v in zip(*GROUPS))
        y = lax.rem(me.y + dy + NY, NY)
        h = jnp.where(e == 1, 1 - me.h, me.h)
        base = (y * 2 + h) * 2
        to_core[p] = term(base + 1 - me.c).astype(BF)
        to_sibling(p).start()
        mine[p] = term(base + me.c)
        return carry

    def both(e, dy):
        p = GROUPS.index((e, dy))
        to_sibling(p).wait_recv()
        return mine[p] + from_core[p].astype(F32)

    def hop(e, dy, value):
        k = HOPS.index((e, dy))
        ring_out[k] = value.astype(BF)
        step = dy if abs(dy) < 3 else (dy - 2 if dy > 0 else dy + 2)
        if dy == 4 and e == 0:
            step = -2
        start(ring_out.at[k], ring_in.at[k], ring_s.at[k], ring_r.at[k], (me.blk(dy=step), me.r))

    def landed(e, dy):
        k = HOPS.index((e, dy))
        arrive(ring_in.at[k], ring_r.at[k])
        return ring_in[k].astype(F32)

    def far_hops(e):
        for sign in (1, -1):
            value = both(e, 2 * sign) + landed(e, 3 * sign)
            if (sign > 0) == (e == 1):
                value += landed(e, 4)
            hop(e, 2 * sign, value)

    def owned(e):
        value = both(e, 0)
        for dy in (1, -1, 2, -2):
            value += landed(e, dy)
        return value

    lax.fori_loop(0, 6, terms, 0, unroll=2)
    for e, dy in GROUPS[:6]:
        hop(e, dy, both(e, dy))
    lax.fori_loop(6, 16, terms, 0, unroll=2)

    w3 = None
    for dx in range(1, NX):
        slot = w3_in.at[lax.rem(me.x + NX - dx, NX)]
        arrive(slot, wx_r.at[dx])
    w3 = sum((w3_in[i].astype(F32) for i in range(1, NX)), w3_in[0].astype(F32))
    zed = me.h * NZ + me.z
    w4_in[zed] = w3.astype(BF)
    for e in (0, 1):
        for dz in range(NZ):
            if e or dz:
                slot = w4_in.at[zed]
                start(slot, slot, wz_s.at[e, dz], wz_r.at[e, dz], (me.blk(e=e), me.rep(dz=dz)))

    far_hops(1)
    for dy in (1, -1):
        hop(1, dy, both(1, dy))
    far_hops(0)
    for dy in (1, -1):
        hop(0, dy, both(0, dy))

    for e in (0, 1):
        for dz in range(NZ):
            if e or dz:
                h = 1 - me.h if e else me.h
                slot = w4_in.at[h * NZ + lax.rem(me.z + NZ - dz, NZ)]
                arrive(slot, wz_r.at[e, dz])
    w4 = sum((w4_in[i].astype(F32) for i in range(1, 2 * NZ)), w4_in[0].astype(F32))
    w5_in[me.y] = w4.astype(BF)

    cross_out[...] = owned(1).astype(BF)
    start(cross_out, cross_in, cross_s.at[0], cross_r.at[0], other)
    for dy in range(1, NY):
        slot = w5_in.at[me.y]
        start(slot, slot, wo_s.at[dy], wo_r.at[dy], (me.blk(dy=dy), me.r))
    value = owned(0)
    for dy in range(1, NY):
        arrive(w5_in.at[lax.rem(me.y + NY - dy, NY)], wo_r.at[dy])
    start(w5_in, w6_in, wa_s.at[1], wa_r.at[1], sibling)
    weight_out[pl.ds(me.c * half, half), :] = w5_in[...].astype(F32).reshape(half, WIDTH)
    arrive(w6_in, wa_r.at[1])
    weight_out[pl.ds((1 - me.c) * half, half), :] = w6_in[...].astype(F32).reshape(half, WIDTH)
    arrive(cross_in, cross_r.at[0])
    grad_out[...] = (value + cross_in[...].astype(F32)).astype(BF)
    for copy in sends:
        copy.wait_send()

    def drain(p, carry):
        to_sibling(p).wait_send()
        return carry

    lax.fori_loop(0, 16, drain, 0)


def dma(*shape):
    return pltpu.SemaphoreType.DMA(shape)


def piece(*lead, dtype=BF):
    return pltpu.VMEM((*lead, SIDE, WIDTH), dtype)


def body(features, tiles, tile_rows, tile_count, weight, cotangent):
    small = pltpu.VMEM((NY, 16, WIDTH), BF)
    return pl.pallas_call(
        layer_kernel,
        out_shape=(
            jax.ShapeDtypeStruct((SIDE, WIDTH), BF),
            jax.ShapeDtypeStruct((SIDE, WIDTH), BF),
            jax.ShapeDtypeStruct((WIDTH, WIDTH), F32),
        ),
        in_specs=[SMEM, SMEM, ANY, ANY, VMEM, ANY],
        out_specs=(VMEM, VMEM, VMEM),
        scratch_shapes=[
            piece(BLOCKS),
            pltpu.VMEM((BLOCKS, SLOTS, SIDE, SIDE), BF),
            pltpu.VMEM((BLOCKS, SIDE, SLOTS * SIDE), BF),
            piece(BLOCKS * SLOTS, dtype=F32),
            piece(BLOCKS * SLOTS + 1),
            piece(PARTS),
            pltpu.VMEM((4, 8, SIDE), jnp.int32),
            pltpu.SMEM((4, 8, SIDE), jnp.int32),
            piece(),
            piece(NZ, 3), piece(NZ), piece(NZ), piece(NZ),
            piece(PARTS + 1),
            piece(16), piece(16), piece(16, dtype=F32),
            piece(len(HOPS)), piece(len(HOPS)),
            piece(), piece(),
            pltpu.VMEM((WIDTH, WIDTH), F32),
            piece(), piece(),
            small, small,
            pltpu.VMEM((NX, 16, WIDTH), BF),
            pltpu.VMEM((2 * NZ, 16, WIDTH), BF),
            small, small,
            dma(4), dma(6, BLOCKS), dma(BLOCKS),
            dma(NZ, 3), dma(NZ, 3), dma(NZ), dma(NZ),
            dma(NZ), dma(NZ), dma(NZ, NX), dma(NZ, NX),
            dma(16), dma(16), dma(len(HOPS)), dma(len(HOPS)),
            dma(1), dma(1), dma(2), dma(2),
            dma(NY), dma(NY), dma(NX), dma(NX), dma(2, NZ), dma(2, NZ), dma(NY), dma(NY),
        ],
        compiler_params=pltpu.CompilerParams(
            collective_id=0, has_side_effects=True, vmem_limit_bytes=58 << 20
        ),
        name="graph_layer",
    )(tile_rows[0, :, 0].T, tile_count[0, :, 0], features, tiles, weight, cotangent)


def solution(mesh):
    placed = (
        P("blk", None),
        P("blk", None, "rep", None, None, None),
        P("blk", None, "rep", None),
        P("blk", None, "rep"),
        P(),
        P("blk", None),
    )
    return jax.shard_map(
        body,
        mesh=mesh,
        in_specs=placed,
        out_specs=(P(("blk", "rep"), None), P(("blk", "rep"), None), P()),
        check_vma=False,
    )
```

```python
import jax
import jax.numpy as jnp
from jax import lax
from jax.experimental import pallas as pl
from jax.experimental.pallas import tpu as pltpu
from jax.sharding import PartitionSpec as P

NX, NY, NZ = 4, 8, 6
SIDE, WIDTH, PARTS, BLOCKS, SLOTS = 128, 256, 24, 32, 4
MESH = pl.DeviceIdType.MESH
BF, F32 = jnp.bfloat16, jnp.float32
VMEM = pl.BlockSpec(memory_space=pltpu.VMEM)
SMEM = pl.BlockSpec(memory_space=pltpu.SMEM)
ANY = pl.BlockSpec(memory_space=pl.ANY)


class Place:
    def __init__(self):
        self.b = lax.axis_index("blk")
        self.r = lax.axis_index("rep")
        self.y = lax.div(self.b, 4)
        self.h = lax.rem(lax.div(self.b, 2), 2)
        self.c = lax.rem(self.b, 2)
        self.z = lax.div(self.r, NX)
        self.x = lax.rem(self.r, NX)

    def blk(self, dy=0, e=0, flip=0):
        y = lax.rem(self.y + dy + NY, NY)
        h = 1 - self.h if e else self.h
        c = 1 - self.c if flip else self.c
        return (y * 2 + h) * 2 + c

    def rep(self, dz=0, dx=0):
        return lax.rem(self.z + dz + NZ, NZ) * NX + lax.rem(self.x + dx + NX, NX)


def greet(peers):
    barrier = pltpu.get_barrier_semaphore()
    for peer in peers:
        pl.semaphore_signal(barrier, inc=1, device_id=peer, device_id_type=MESH)
    pl.semaphore_wait(barrier, len(peers))


def remote(src, dst, send_sem, recv_sem, device):
    return pltpu.make_async_remote_copy(
        src_ref=src, dst_ref=dst, send_sem=send_sem, recv_sem=recv_sem,
        device_id=device, device_id_type=MESH,
    )


HOPS = [(e, dy) for dy in (4, 3, -3, 2, -2, 1, -1) for e in (1, 0)]
GROUPS = [(1, 4), (0, 4)] + [(e, s * m) for m in (3, 2, 1) for s in (1, -1) for e in (1, 0)] + [(1, 0), (0, 0)]


def choose(at, values):
    out = values[0]
    for i, value in enumerate(values[1:], 1):
        out = jnp.where(at == i, value, out)
    return out


def layer_kernel(
    rows, counts, feat, tiles_hbm, weight, cot_hbm,
    act_out, grad_out, weight_out,
    feats, tiles, tiles_t, prods, sums, part, marks, marks_s, cot,
    got_x, mid_x, sum_z, got_z, back, to_core, from_core, mine, ring_out, ring_in,
    cross_out, cross_in, wsum, w1_out, w1_in, w2_out, w2_in, w3_in, w4_in, w5_in, w6_in,
    local_sem, feat_s, feat_r, rx_s, rx_r, rz_s, rz_r, gz_s, gz_r, gx_s, gx_r, core_s, core_r, ring_s, ring_r,
    cross_s, cross_r, wa_s, wa_r, wy_s, wy_r, wx_s, wx_r, wz_s, wz_r, wo_s, wo_r,
):
    me = Place()
    sibling = (me.blk(flip=1), me.r)
    other = (me.blk(e=1), me.r)
    far = me.rep(dz=3)
    peers = [sibling]
    peers += [(me.blk(dy=dy), me.r) for dy in range(1, NY)]
    peers += [(me.b, me.rep(dx=dx)) for dx in range(1, NX)]
    peers += [(me.blk(e=e), me.rep(dz=dz)) for e in (0, 1) for dz in range(NZ) if e or dz]

    load_tiles = pltpu.make_async_copy(tiles_hbm.at[0, :, 0], tiles, local_sem.at[0])
    load_tiles.start()
    load_cot = pltpu.make_async_copy(cot_hbm.at[pl.ds(me.r * SIDE, SIDE), :], cot, local_sem.at[1])
    load_cot.start()
    own = feat.at[pl.ds(me.r * SIDE, SIDE), :]
    load_own = pltpu.make_async_copy(own, feats.at[me.b], local_sem.at[2])
    load_own.start()
    greet(peers)
    sends = []

    def start(*args):
        copy = remote(*args)
        copy.start()
        sends.append(copy)

    def arrive(dst, sem):
        remote(dst, dst, local_sem.at[3], sem, sibling).wait_recv()

    def feat_send(src, slot, lane, device):
        start(src, feats.at[slot], feat_s.at[lane, slot], feat_r.at[slot], device)

    def feat_arrive(slot):
        arrive(feats.at[slot], feat_r.at[slot])

    def feat_spread(src, slot):
        for n, dy in enumerate((2, -2, 1, -1)):
            feat_send(src, slot, n, (me.blk(dy=dy), me.r))
        feat_send(src, slot, 4, sibling)

    feat_send(feat.at[pl.ds(far * SIDE, SIDE), :], me.b, 5, (me.blk(e=1), far))
    feat_spread(own, me.b)

    lane = lax.broadcasted_iota(jnp.int32, (8, SIDE), 1)
    nought = jnp.zeros((8, SIDE), jnp.int32)

    def target(c, k):
        return jnp.where(k < counts[c], rows[k, c], PARTS)

    def slot_key(s):
        return target(lax.div(s, SLOTS), lax.rem(s, SLOTS))

    def spread(s, carry):
        unique, below, upto = carry
        key = slot_key(s)
        unique = jnp.where(lane == s, key * SIDE + s, unique)
        below += jnp.where(lane > key, 1, 0)
        upto += jnp.where(lane >= key, 1, 0)
        return unique, below, upto

    def rank_of(s, rank):
        return rank + jnp.where(unique > slot_key(s) * SIDE + s, 1, 0)

    def place(s, carry):
        order, keys = carry
        hit = lane == marks_s[0, 0, s]
        return jnp.where(hit, s, order), jnp.where(hit, slot_key(s), keys)

    sums[SIDE] = jnp.zeros((SIDE, WIDTH), BF)
    back[PARTS] = jnp.zeros((SIDE, WIDTH), BF)

    def turn(lo, hi):
        def body(c, carry):
            tiles_t[c] = tiles[c].reshape(SLOTS * SIDE, SIDE).T
            return carry

        lax.fori_loop(lo, hi, body, 0)

    def column(c):
        value = jnp.dot(tiles[c].reshape(SLOTS * SIDE, SIDE), feats[c], preferred_element_type=F32)
        prods[pl.ds(c * SLOTS, SLOTS)] = value.reshape(SLOTS, SIDE, WIDTH)

    def columns(which, flip):
        def body(j, carry):
            e, dy = (choose(j, v) for v in zip(*which))
            y = lax.rem(me.y + dy + NY, NY)
            h = jnp.where(e == 1, 1 - me.h, me.h)
            c = (y * 2 + h) * 2 + (1 - me.c if flip else me.c)
            if flip:
                feat_arrive(c)
            column(c)
            return carry

        lax.fori_loop(0, len(which), body, 0, unroll=2)

    def onward(e):
        for dy in (-2, 2):
            slot = me.blk(dy=dy, e=e)
            feat_arrive(slot)
            if (dy < 0) == (e == 1):
                feat_send(feats.at[slot], slot, 1 if dy > 0 else 0, (me.blk(dy=-dy), me.r))
            step = -1 if dy > 0 else 1
            feat_send(feats.at[slot], slot, 2, (me.blk(dy=step), me.r))
            feat_send(feats.at[slot], slot, 4, sibling)

    def settle(e, *dys):
        for dy in dys:
            slot = me.blk(dy=dy, e=e)
            feat_arrive(slot)
            feat_send(feats.at[slot], slot, 4, sibling)

    unique, below, upto = lax.fori_loop(0, SIDE, spread, (nought, nought, nought), unroll=8)
    onward(0)
    crossed = me.blk(e=1)
    feat_arrive(crossed)
    feat_spread(feats.at[crossed], crossed)
    settle(0, 1, -1)
    marks[0] = lax.fori_loop(0, SIDE, rank_of, nought, unroll=8)
    marks[3] = jnp.where(upto > below, upto - 1, SIDE)
    pltpu.sync_copy(marks.at[0], marks_s.at[0])
    load_tiles.wait()
    load_own.wait()
    first = [(0, 0), (1, 0)] + [(0, dy) for dy in (1, -1, 2, -2)]
    second = [(1, dy) for dy in (1, -1, 2, -2)] + [(0, dy) for dy in (3, -3, 4)]
    last = [(1, dy) for dy in (3, -3, 4)]
    columns(first, 0)
    onward(1)
    settle(1, 1, -1)
    settle(0, 3, -3, 4)
    order, keys = lax.fori_loop(0, SIDE, place, (nought, nought), unroll=8)
    marks[1] = order
    marks[2] = keys
    pltpu.sync_copy(marks.at[pl.ds(1, 3)], marks_s.at[pl.ds(1, 3)])
    columns(first, 1)
    columns(second, 0)
    settle(1, 3, -3, 4)
    columns(second, 1)
    columns(last, 0)
    columns(last, 1)

    for lo in range(0, SIDE, 64):
        span = slice(lo, lo + 64)

        def scan(p, total):
            key = marks_s[2, 0, p]
            before = marks_s[2, 0, jnp.maximum(p - 1, 0)]
            keep = jnp.where(key == before, 1.0, 0.0).astype(F32)
            total = total * keep + prods[marks_s[1, 0, p], span, :]
            sums[p, span, :] = total.astype(BF)
            return total

        lax.fori_loop(0, SIDE, scan, jnp.zeros((64, WIDTH), F32), unroll=4)

    def pick(t):
        part[t] = sums[marks_s[3, 0, t]]

    run, spot = lax.div(me.z, 3), lax.rem(me.z, 3)

    def place_z(j, across):
        return (1 - run if across else run) * 3 + lax.rem(spot + j, 3)

    at_z = [place_z(1, 1), place_z(2, 1), place_z(0, 1), place_z(1, 0), place_z(2, 0), me.z]

    def along(z):
        return (me.b, z * NX + me.x)

    def tile_at(k, dx=0):
        return at_z[k] * NX + lax.rem(me.x + dx + NX, NX)

    def ways(k):
        return 1 if k % 2 == 0 else -1

    def toward(dx):
        return (me.b, me.rep(dx=dx))

    for k in range(NZ):
        pick(tile_at(k, 2))
        start(part.at[tile_at(k, 2)], got_x.at[k, 0], rx_s.at[k, 0], rx_r.at[k, 0], toward(ways(k)))
    for k in range(NZ):
        for dx in (0, 1, -1):
            pick(tile_at(k, dx))

    def pass_on(k):
        arrive(got_x.at[k, 0], rx_r.at[k, 0])
        mid_x[k] = (got_x[k, 0].astype(F32) + part[tile_at(k, ways(k))].astype(F32)).astype(BF)
        start(mid_x.at[k], got_x.at[k, 1], rx_s.at[k, 1], rx_r.at[k, 1], toward(ways(k)))
        start(part.at[tile_at(k, -ways(k))], got_x.at[k, 2], rx_s.at[k, 2], rx_r.at[k, 2],
              toward(-ways(k)))

    def sum_x(k):
        arrive(got_x.at[k, 1], rx_r.at[k, 1])
        arrive(got_x.at[k, 2], rx_r.at[k, 2])
        value = part[tile_at(k)].astype(F32) + got_x[k, 1].astype(F32) + got_x[k, 2].astype(F32)
        if k in (0, 1, 3, 4):
            z_send(k, value, place_z(k % 3 + 1, 0))
        return value

    def z_send(k, value, z):
        sum_z[k] = value.astype(BF)
        start(sum_z.at[k], got_z.at[k], rz_s.at[k], rz_r.at[k], along(z))

    def z_got(k):
        arrive(got_z.at[k], rz_r.at[k])
        return got_z[k].astype(F32)

    totals = {}
    for k in range(NZ):
        pass_on(k)
    for k in range(NZ):
        totals[k] = sum_x(k)
        if k == 3:
            z_send(2, totals[2] + z_got(0) + z_got(1), place_z(0, 1))
    turn(0, BLOCKS // 2)
    value = totals[NZ - 1]
    for k in (3, 4, 2):
        value += z_got(k)

    load_cot.wait()
    agg = value.astype(BF)
    pre = jnp.dot(agg, weight[...], preferred_element_type=F32)
    sig = jax.nn.sigmoid(pre)
    dpre = (cot[...].astype(F32) * sig * (1.0 + pre * (1.0 - sig))).astype(BF)
    back[me.r] = lax.dot_general(
        dpre, weight[...], (((1,), (1,)), ((), ())), preferred_element_type=F32
    ).astype(BF)

    at_z = [me.z, place_z(1, 0), place_z(2, 0), place_z(0, 1), place_z(1, 1), place_z(2, 1)]

    def over_x(k):
        slot = back.at[tile_at(k)]
        for dx in (1, -1):
            start(slot, slot, gx_s.at[k, dx % NX], gx_r.at[k, dx % NX], toward(dx))

    def relay(k):
        way = ways(k)
        slot = back.at[tile_at(k, -way)]
        arrive(slot, gx_r.at[k, way % NX])
        start(slot, slot, gx_s.at[k, 2], gx_r.at[k, 2], toward(way))

    mine_back = back.at[me.r]
    for k in (3, 2, 1):
        start(mine_back, mine_back, gz_s.at[k], gz_r.at[me.z], along(at_z[k]))
    over_x(0)

    act_out[...] = (pre * sig).astype(BF)
    wsum[...] = lax.dot_general(agg, dpre, (((0,), (0,)), ((), ())), preferred_element_type=F32)
    half = SIDE
    w1_out[...] = wsum[pl.ds((1 - me.c) * half, half), :].astype(BF)
    start(w1_out, w1_in, wa_s.at[0], wa_r.at[0], sibling)

    def from_z(k):
        slot = back.at[tile_at(k)]
        arrive(slot, gz_r.at[at_z[k]])
        if k == 3:
            for j in (2, 1):
                start(slot, slot, gz_s.at[3 + j], gz_r.at[at_z[k]], along(at_z[j]))
        over_x(k)

    for k in (3, 1, 2):
        from_z(k)
    relay(0)
    arrive(w1_in, wa_r.at[0])
    w1 = wsum[pl.ds(me.c * half, half), :] + w1_in[...].astype(F32)
    wsum[0:half, :] = w1
    w2_out[...] = w1.astype(BF).reshape(NY, 16, WIDTH)
    for dy in range(1, NY):
        start(w2_out.at[lax.rem(me.y + dy, NY)], w2_in.at[dy], wy_s.at[dy], wy_r.at[dy],
              (me.blk(dy=dy), me.r))
    turn(BLOCKS // 2, 3 * BLOCKS // 4)
    for k in (4, 5):
        from_z(k)
    for k in (1, 2, 3):
        relay(k)
    w2 = wsum[pl.ds(me.y * 16, 16), :]
    for dy in range(1, NY):
        arrive(w2_in.at[dy], wy_r.at[dy])
        w2 += w2_in[dy].astype(F32)
    w3_in[me.x] = w2.astype(BF)
    for dx in range(1, NX):
        slot = w3_in.at[me.x]
        start(slot, slot, wx_s.at[dx], wx_r.at[dx], (me.b, me.rep(dx=dx)))

    turn(3 * BLOCKS // 4, BLOCKS)
    for k in (4, 5):
        relay(k)

    for dx in range(1, NX):
        slot = w3_in.at[lax.rem(me.x + NX - dx, NX)]
        arrive(slot, wx_r.at[dx])
    w3 = sum((w3_in[i].astype(F32) for i in range(1, NX)), w3_in[0].astype(F32))
    zed = me.h * NZ + me.z
    w4_in[zed] = w3.astype(BF)
    for e in (0, 1):
        for dz in range(NZ):
            if e or dz:
                slot = w4_in.at[zed]
                start(slot, slot, wz_s.at[e, dz], wz_r.at[e, dz], (me.blk(e=e), me.rep(dz=dz)))

    for k in range(NZ):
        arrive(back.at[tile_at(k, ways(k))], gx_r.at[k, -ways(k) % NX])
        arrive(back.at[tile_at(k, 2)], gx_r.at[k, 2])

    def term(c):
        picked = jnp.concatenate([back[target(c, k)] for k in range(SLOTS)], axis=0)
        return jnp.dot(tiles_t[c], picked, preferred_element_type=F32)

    def to_sibling(p):
        return remote(to_core.at[p], from_core.at[p], core_s.at[p], core_r.at[p], sibling)

    def terms(p, carry):
        e, dy = (choose(p, v) for v in zip(*GROUPS))
        y = lax.rem(me.y + dy + NY, NY)
        h = jnp.where(e == 1, 1 - me.h, me.h)
        base = (y * 2 + h) * 2
        to_core[p] = term(base + 1 - me.c).astype(BF)
        to_sibling(p).start()
        mine[p] = term(base + me.c)
        return carry

    def both(e, dy):
        p = GROUPS.index((e, dy))
        to_sibling(p).wait_recv()
        return mine[p] + from_core[p].astype(F32)

    def hop(e, dy, value):
        k = HOPS.index((e, dy))
        ring_out[k] = value.astype(BF)
        step = dy if abs(dy) < 3 else (dy - 2 if dy > 0 else dy + 2)
        if dy == 4 and e == 0:
            step = -2
        start(ring_out.at[k], ring_in.at[k], ring_s.at[k], ring_r.at[k], (me.blk(dy=step), me.r))

    def landed(e, dy):
        k = HOPS.index((e, dy))
        arrive(ring_in.at[k], ring_r.at[k])
        return ring_in[k].astype(F32)

    def far_hops(e):
        for sign in (1, -1):
            value = both(e, 2 * sign) + landed(e, 3 * sign)
            if (sign > 0) == (e == 1):
                value += landed(e, 4)
            hop(e, 2 * sign, value)

    def owned(e):
        value = both(e, 0)
        for dy in (1, -1, 2, -2):
            value += landed(e, dy)
        return value

    lax.fori_loop(0, 6, terms, 0, unroll=2)
    for e, dy in GROUPS[:6]:
        hop(e, dy, both(e, dy))
    lax.fori_loop(6, 16, terms, 0, unroll=2)

    far_hops(1)
    for dy in (1, -1):
        hop(1, dy, both(1, dy))
    far_hops(0)
    for dy in (1, -1):
        hop(0, dy, both(0, dy))
    for e in (0, 1):
        for dz in range(NZ):
            if e or dz:
                h = 1 - me.h if e else me.h
                slot = w4_in.at[h * NZ + lax.rem(me.z + NZ - dz, NZ)]
                arrive(slot, wz_r.at[e, dz])
    w4 = sum((w4_in[i].astype(F32) for i in range(1, 2 * NZ)), w4_in[0].astype(F32))
    w5_in[me.y] = w4.astype(BF)
    for dy in range(1, NY):
        slot = w5_in.at[me.y]
        start(slot, slot, wo_s.at[dy], wo_r.at[dy], (me.blk(dy=dy), me.r))

    cross_out[...] = owned(1).astype(BF)
    start(cross_out, cross_in, cross_s.at[0], cross_r.at[0], other)
    value = owned(0)
    for dy in range(1, NY):
        arrive(w5_in.at[lax.rem(me.y + NY - dy, NY)], wo_r.at[dy])
    start(w5_in, w6_in, wa_s.at[1], wa_r.at[1], sibling)
    weight_out[pl.ds(me.c * half, half), :] = w5_in[...].astype(F32).reshape(half, WIDTH)
    arrive(w6_in, wa_r.at[1])
    weight_out[pl.ds((1 - me.c) * half, half), :] = w6_in[...].astype(F32).reshape(half, WIDTH)
    arrive(cross_in, cross_r.at[0])
    grad_out[...] = (value + cross_in[...].astype(F32)).astype(BF)
    for copy in sends:
        copy.wait_send()

    def drain(p, carry):
        to_sibling(p).wait_send()
        return carry

    lax.fori_loop(0, 16, drain, 0)


def dma(*shape):
    return pltpu.SemaphoreType.DMA(shape)


def piece(*lead, dtype=BF):
    return pltpu.VMEM((*lead, SIDE, WIDTH), dtype)


def body(features, tiles, tile_rows, tile_count, weight, cotangent):
    small = pltpu.VMEM((NY, 16, WIDTH), BF)
    return pl.pallas_call(
        layer_kernel,
        out_shape=(
            jax.ShapeDtypeStruct((SIDE, WIDTH), BF),
            jax.ShapeDtypeStruct((SIDE, WIDTH), BF),
            jax.ShapeDtypeStruct((WIDTH, WIDTH), F32),
        ),
        in_specs=[SMEM, SMEM, ANY, ANY, VMEM, ANY],
        out_specs=(VMEM, VMEM, VMEM),
        scratch_shapes=[
            piece(BLOCKS),
            pltpu.VMEM((BLOCKS, SLOTS, SIDE, SIDE), BF),
            pltpu.VMEM((BLOCKS, SIDE, SLOTS * SIDE), BF),
            piece(BLOCKS * SLOTS, dtype=F32),
            piece(BLOCKS * SLOTS + 1),
            piece(PARTS),
            pltpu.VMEM((4, 8, SIDE), jnp.int32),
            pltpu.SMEM((4, 8, SIDE), jnp.int32),
            piece(),
            piece(NZ, 3), piece(NZ), piece(NZ), piece(NZ),
            piece(PARTS + 1),
            piece(16), piece(16), piece(16, dtype=F32),
            piece(len(HOPS)), piece(len(HOPS)),
            piece(), piece(),
            pltpu.VMEM((WIDTH, WIDTH), F32),
            piece(), piece(),
            small, small,
            pltpu.VMEM((NX, 16, WIDTH), BF),
            pltpu.VMEM((2 * NZ, 16, WIDTH), BF),
            small, small,
            dma(4), dma(6, BLOCKS), dma(BLOCKS),
            dma(NZ, 3), dma(NZ, 3), dma(NZ), dma(NZ),
            dma(NZ), dma(NZ), dma(NZ, NX), dma(NZ, NX),
            dma(16), dma(16), dma(len(HOPS)), dma(len(HOPS)),
            dma(1), dma(1), dma(2), dma(2),
            dma(NY), dma(NY), dma(NX), dma(NX), dma(2, NZ), dma(2, NZ), dma(NY), dma(NY),
        ],
        compiler_params=pltpu.CompilerParams(
            collective_id=0, has_side_effects=True, vmem_limit_bytes=58 << 20
        ),
        name="graph_layer",
    )(tile_rows[0, :, 0].T, tile_count[0, :, 0], features, tiles, weight, cotangent)


def solution(mesh):
    placed = (
        P("blk", None),
        P("blk", None, "rep", None, None, None),
        P("blk", None, "rep", None),
        P("blk", None, "rep"),
        P(),
        P("blk", None),
    )
    return jax.shard_map(
        body,
        mesh=mesh,
        in_specs=placed,
        out_specs=(P(("blk", "rep"), None), P(("blk", "rep"), None), P()),
        check_vma=False,
    )
```
